32 devices in a mesh: tm: 8 (over z, x), chan: 4 (over y, core).
Axes of the slice: x: 2, y: 2, z: 4, core: 2. Of those that a mesh axis runs over, the one named last changes fastest.
Arguments:
- data: bfloat16 [1024, 10240], P('chan', 'tm'), may hold values from -80 to 80
- templates: bfloat16 [1024, 102400], P('tm', 'chan'), may hold values from -6 to 6
- valid: int32 [1024, 1024], P('tm', 'chan'), may hold values from 0 to 1, as said below
Outputs:
- detection: float32 [3, 128, 10240], P(None, 'chan', 'tm')
The draws below stay inside these ranges and needn't reach their ends.
Inputs may be any that keep to these rules, and one draw needn't show every extreme that they name: `valid`: template number r uses channel r mod 1024.
All inputs are finite; a program needn't handle non-finite values.
Results may differ from the reference program's by a relative error of at most 0.0003.
Values may be sent and summed in bfloat16 or wider, within the bound.
No kernel may reach another device: no remote copies, remote signals or barrier semaphores. Data moves between devices by JAX's collectives and lax.ppermute only.
A program may use at most 128 MiB of HBM per device.

```python
import math
import jax
import jax.numpy as jnp
from jax import lax

CHANNELS = 1024
TLEN = 100
BLOCK = 128
WINDOW = 3
SLAB = 1280
TEMPLATES = 1024
TIME = 10240
N_TM = 8


def draw_data(key, part):
    key = jax.random.fold_in(key, 11)
    first, second = jax.random.split(key, 2)
    position = jnp.arange(CHANNELS, dtype=jnp.float32) / (CHANNELS - 1)
    rough = jax.random.uniform(second, (CHANNELS,), minval=0.6, maxval=1.5)
    gain = jnp.exp(position * math.log(3.0)) * rough
    values = jax.random.truncated_normal(first, -5.0, 5.0, (CHANNELS, TIME)) * gain[:, None]
    return values.astype(jnp.bfloat16)


def draw_valid(key, part):
    key = jax.random.fold_in(key, 23)
    levels = 30 + 60 * jnp.arange(CHANNELS, dtype=jnp.int32) // CHANNELS
    rolls = jax.random.randint(key, (TEMPLATES, CHANNELS), 0, 100)
    forced = jnp.arange(TEMPLATES, dtype=jnp.int32)[:, None] % CHANNELS == jnp.arange(CHANNELS, dtype=jnp.int32)[None, :]
    return jnp.where((rolls < levels[None, :]) | forced, 1, 0).astype(jnp.int32)


def steps_of(key, shape, pieces, low, top_value):
    factor_of, own = 1.0, jax.random.fold_in(key, 6)
    for axis_at, blocks in pieces:
        steps = jnp.exp(jax.random.uniform(jax.random.fold_in(own, axis_at), (blocks,), jnp.float32, low / len(pieces), top_value / len(pieces)))
        factor_of = factor_of * jnp.repeat(steps, shape[axis_at] // blocks).reshape([-1 if axis == axis_at else 1 for axis in range(len(shape))])
    return factor_of


def bell_draw(key, shape, width, bound, shards=(), kind=jnp.bfloat16):
    values = jax.random.normal(key, shape, jnp.float32) * width
    if len(shards) > 0:
        values = steps_of(key, shape, shards, -0.22, 0.18) * values
    return jnp.clip(values, min=-bound, max=bound).astype(kind)


def setup_inputs(seed: int = 0) -> dict:
    keys = jax.random.split(jax.random.key(seed), 4)
    data = draw_data(jax.random.fold_in(keys[3], 71), 0)
    templates = bell_draw(keys[1], (TEMPLATES, CHANNELS * TLEN), 1.0, 6.0, ((0, 8), (1, 4)))
    valid = draw_valid(jax.random.fold_in(keys[3], 71), 0)
    return {"data": data, "templates": templates, "valid": valid}


EPSILON = 1e-06

def finish(num, esum, tnorm, count):
    scale = jnp.sqrt(count * TLEN)
    return num * scale[..., None] * lax.rsqrt(esum * tnorm[..., None] + EPSILON)

def reference(data, templates, valid):
    mask = valid.astype(jnp.float32)
    padded = jnp.pad(data.astype(jnp.float32), ((0, 0), (0, TLEN - 1)))
    energy = lax.reduce_window(jnp.square(padded), jnp.float32(0.0), lax.add, (1, TLEN), (1, 1), 'VALID')

    def per_slab(index):
        blocks = (index + jnp.arange(WINDOW, dtype=jnp.int32)) % N_TM
        rows = (blocks[:, None] * BLOCK + jnp.arange(BLOCK, dtype=jnp.int32)[None, :]).reshape(-1)
        chosen = jnp.take(templates, rows, axis=0).astype(jnp.float32).reshape(WINDOW * BLOCK, CHANNELS, TLEN)
        weights = jnp.take(mask, rows, axis=0)
        kernel = chosen * weights[:, :, None]
        start = (index * SLAB).astype(jnp.int32)
        zero = jnp.zeros((), jnp.int32)
        segment = lax.dynamic_slice(padded, (zero, start), (CHANNELS, SLAB + TLEN - 1))
        num = lax.conv_general_dilated(segment[None], kernel, (1,), 'VALID', dimension_numbers=('NCH', 'OIH', 'NCH'), precision=lax.Precision.HIGHEST)[0]
        part = lax.dynamic_slice(energy, (zero, start), (CHANNELS, SLAB))
        esum = jnp.dot(weights, part, precision=lax.Precision.HIGHEST)
        tnorm = lax.optimization_barrier(jnp.sum(jnp.square(kernel), axis=(1, 2)))
        count = lax.optimization_barrier(jnp.sum(weights, axis=1))
        return finish(num, esum, tnorm, count).reshape(WINDOW, BLOCK, SLAB)
    result = lax.map(per_slab, jnp.arange(N_TM, dtype=jnp.int32))
    return jnp.transpose(result, (1, 2, 0, 3)).reshape(WINDOW, BLOCK, N_TM * SLAB)
```

```python
import jax, jax.numpy as jnp
from jax import lax
from jax.experimental import pallas as pl
from jax.experimental.pallas import tpu as pltpu
from jax.sharding import PartitionSpec as P

TLEN = 100
EPSILON = 1e-06
SIDE = 16
STEP = 32
EDGE = 128
LIMIT = 56 * 1024 * 1024
PAIRS = (TLEN + 2) // 2
TAPS = 2 * PAIRS + 1
Q = 17

VMEM = pl.BlockSpec(memory_space=pltpu.VMEM)
SMEM = pl.BlockSpec(memory_space=pltpu.SMEM)
ANY = pl.BlockSpec(memory_space=pl.ANY)


def relayout(t_hbm, v_ref, w, t_all, tall, mask, arrived):
    chans = v_ref.shape[1]
    steps = chans // STEP
    wide = STEP * TLEN
    mask[...] = v_ref[...].astype(jnp.float32).T
    blank = jnp.zeros(w.shape[1:], w.dtype)
    w[0] = blank
    for tap in range(TLEN + 1, TAPS):
        w[tap] = blank

    def step(i, total):
        columns = pl.ds(pl.multiple_of(i * wide, wide), wide)
        channels = pl.ds(pl.multiple_of(i * STEP, STEP), STEP)
        pltpu.make_async_copy(t_hbm.at[:, columns], t_all.at[:, columns], arrived.at[i]).wait()
        tall[...] = t_all[:, columns].T.astype(jnp.float32)
        keep = mask[channels, :]

        def tap(l, total):
            kernel = tall[pl.ds(l, STEP, stride=TLEN), :] * keep
            w[l + 1, channels, :] = kernel.astype(w.dtype)
            return total + kernel * kernel

        return lax.fori_loop(0, TLEN, tap, total, unroll=10)

    total = lax.fori_loop(0, steps, step, jnp.zeros((STEP, w.shape[2]), jnp.float32))
    norm = jnp.sum(total, axis=0, keepdims=True)
    return jnp.broadcast_to(norm, (128, norm.shape[1])).T


def interleave(x_ref, h_ref, turned, windows):
    chans, slab = x_ref.shape
    lanes = turned.shape[2]
    reach = windows.shape[0] // SIDE
    step = slab // SIDE
    for b in range(turned.shape[0]):
        rows = slice(b * lanes, min((b + 1) * lanes, chans))
        n = rows.stop - rows.start
        turned[b, :slab, :n] = x_ref[rows, :].T.astype(jnp.float32)
        turned[b, slab:, :n] = h_ref[rows, :].T.astype(jnp.float32)
    for a in range(reach):
        for p in range(2):
            for b in range(turned.shape[0]):
                n = min(lanes, chans - b * lanes)
                samples = turned[b, pl.ds(2 * a + p, SIDE, stride=step), :]
                at = p * chans + b * lanes
                windows[a * SIDE:(a + 1) * SIDE, at:at + n] = samples[:, :n].astype(windows.dtype)


def correlate(w, windows, acc, flat, before):
    half, rows = acc.shape[1:]
    acc[...] = jnp.zeros_like(acc)

    def group(g, carry):
        before(g)
        left, right = [], []
        for k in range(Q):
            q = g * Q + k
            left.append(windows[pl.ds(pl.multiple_of(q * SIDE, SIDE), half), :])
            for m in (2 * q, 2 * q + 1):
                right.append(jnp.concatenate([w[m + 1], w[m]], axis=1))
        d = jnp.dot(jnp.concatenate(left, axis=1), jnp.concatenate(right, axis=0), preferred_element_type=jnp.float32)
        for r in range(2):
            acc[r] += d[:, r * rows:(r + 1) * rows]
        return carry

    lax.fori_loop(0, PAIRS // Q, group, 0)
    inner = half // SIDE
    step = 2 * inner
    for r in range(2):
        for b in range(SIDE):
            flat[pl.ds(step * b + r, inner, stride=2), :] = acc[r, pl.ds(b, inner, stride=SIDE), :]


def split(whole, mine, keep_ref, give_ref):
    pieces, piece = keep_ref.shape[:2]
    for i in range(pieces):
        at = pl.multiple_of((2 * i + mine) * piece, piece)
        keep_ref[i] = whole[pl.ds(at, piece), :]
        at = pl.multiple_of((2 * i + 1 - mine) * piece, piece)
        give_ref[i] = whole[pl.ds(at, piece), :]


def first_kernel(bit_ref, t_hbm, v_ref, v1_ref, v2_ref, x_ref, h_ref,
                 w_hbm, keep_ref, give_ref, skeep_ref, sgive_ref,
                 w, t_all, tall, mask, turned, windows, acc, flat, whole, power, arrived, left):
    chans, slab = x_ref.shape
    wide = STEP * TLEN
    for i in range(chans // STEP):
        columns = pl.ds(i * wide, wide)
        pltpu.make_async_copy(t_hbm.at[:, columns], t_all.at[:, columns], arrived.at[i]).start()
    interleave(x_ref, h_ref, turned, windows)
    norm = relayout(t_hbm, v_ref, w, t_all, tall, mask, arrived)
    out = pltpu.make_async_copy(w, w_hbm, left)
    out.start()
    mine = bit_ref[0]
    valids = [r[...].astype(jnp.bfloat16) for r in (v_ref, v1_ref, v2_ref)]
    for at in range(0, slab + EDGE, 128):
        part = x_ref[:, at:at + 128] if at < slab else h_ref[:, at - slab:at - slab + 128]
        square = jnp.square(part.astype(jnp.float32))
        high = square.astype(jnp.bfloat16)
        low = (square - high.astype(jnp.float32)).astype(jnp.bfloat16)
        for j in range(3):
            power[j, :, at:at + 128] = jnp.dot(valids[j], high, preferred_element_type=jnp.float32) + jnp.dot(valids[j], low, preferred_element_type=jnp.float32)
    for j in range(3):
        count = jnp.sum(valids[j].astype(jnp.float32), axis=1, keepdims=True)
        lane = lax.broadcasted_iota(jnp.int32, norm.shape, 1)
        power[j, :, slab + EDGE:] = jnp.where(lane < 64, count, norm)
    for j in range(3):
        split(power.at[j], mine, skeep_ref.at[j], sgive_ref.at[j])
    correlate(w, windows, acc, flat, lambda g: None)
    whole[...] = flat[...].T
    split(whole, mine, keep_ref, give_ref)
    out.wait()


def later_kernel(bit_ref, w_hbm, x_ref, next_hbm, keep_ref, give_ref, h_ref, w, turned, windows, acc, flat, whole, arrived):
    groups = PAIRS // Q

    def piece(g):
        lo = g * 2 * Q
        return pltpu.make_async_copy(w_hbm.at[pl.ds(lo, 2 * Q)], w.at[pl.ds(lo, 2 * Q)], arrived.at[g])

    for g in range(groups):
        piece(g).start()
    last = pltpu.make_async_copy(w_hbm.at[pl.ds(TAPS - 1, 1)], w.at[pl.ds(TAPS - 1, 1)], arrived.at[groups])
    last.start()
    edge = pltpu.make_async_copy(next_hbm.at[:, pl.ds(0, EDGE)], h_ref, arrived.at[groups + 1])
    edge.start()
    edge.wait()
    h_ref[...] = h_ref[...] * bit_ref[1].astype(jnp.bfloat16)
    interleave(x_ref, h_ref, turned, windows)
    last.wait()
    piece(0).wait()

    def before(g):
        @pl.when(g + 1 < groups)
        def _():
            piece(g + 1).wait()

    correlate(w, windows, acc, flat, before)
    whole[...] = flat[...].T
    split(whole, bit_ref[0], keep_ref, give_ref)


def sizes(chans, slab, rows):
    half = slab // 2
    lanes = 128
    blocks = -(-chans // lanes)
    reach = half // SIDE + PAIRS - 1
    return [
        pltpu.VMEM((blocks, slab + EDGE, lanes), jnp.float32),
        pltpu.VMEM((reach * SIDE, 2 * chans), jnp.bfloat16),
        pltpu.VMEM((2, half, rows), jnp.float32),
        pltpu.VMEM((slab, rows), jnp.float32),
        pltpu.VMEM((rows, slab), jnp.float32),
    ]


def first(bit, templates, valid, valid1, valid2, x, h, pieces):
    chans, slab = x.shape
    rows = templates.shape[0]
    piece = rows // pieces
    f32, bf16 = jnp.float32, jnp.bfloat16
    wide = slab + EDGE + 128
    return pl.pallas_call(
        first_kernel,
        in_specs=[SMEM, ANY] + [VMEM] * 5,
        out_specs=[ANY] + [VMEM] * 4,
        out_shape=[
            jax.ShapeDtypeStruct((TAPS, chans, rows), bf16),
            jax.ShapeDtypeStruct((pieces // 2, piece, slab), f32),
            jax.ShapeDtypeStruct((pieces // 2, piece, slab), f32),
            jax.ShapeDtypeStruct((3, pieces // 2, piece, wide), f32),
            jax.ShapeDtypeStruct((3, pieces // 2, piece, wide), f32),
        ],
        scratch_shapes=[
            pltpu.VMEM((TAPS, chans, rows), bf16),
            pltpu.VMEM((rows, chans * TLEN), bf16),
            pltpu.VMEM((STEP * TLEN, rows), f32),
            pltpu.VMEM((chans, rows), f32),
        ] + sizes(chans, slab, rows) + [
            pltpu.VMEM((3, rows, wide), f32),
            pltpu.SemaphoreType.DMA((chans // STEP,)),
            pltpu.SemaphoreType.DMA,
        ],
        compiler_params=pltpu.CompilerParams(vmem_limit_bytes=LIMIT),
        cost_estimate=pl.CostEstimate(flops=2 * rows * chans * TLEN * slab, bytes_accessed=4 * rows * chans * TLEN, transcendentals=0),
    )(bit, templates, valid, valid1, valid2, x, h)


def later(bit, w, x, follows, pieces):
    chans, slab = x.shape
    rows = w.shape[2]
    piece = rows // pieces
    f32 = jnp.float32
    return pl.pallas_call(
        later_kernel,
        in_specs=[SMEM, ANY, VMEM, ANY],
        out_specs=[VMEM] * 2,
        out_shape=[jax.ShapeDtypeStruct((pieces // 2, piece, slab), f32)] * 2,
        scratch_shapes=[pltpu.VMEM((chans, EDGE), x.dtype), pltpu.VMEM(w.shape, w.dtype)] + sizes(chans, slab, rows) + [pltpu.SemaphoreType.DMA((PAIRS // Q + 2,))],
        compiler_params=pltpu.CompilerParams(vmem_limit_bytes=LIMIT),
        cost_estimate=pl.CostEstimate(flops=2 * rows * chans * TLEN * slab, bytes_accessed=2 * rows * chans * TLEN, transcendentals=0),
    )(bit, w, x, follows)


def window_kernel(p_ref, esum_ref):
    slab = esum_ref.shape[2]
    wide = slab + EDGE
    for j in range(p_ref.shape[0]):
        sums = {1: p_ref[j, :, :wide]}
        for reach in (1, 2, 4, 8, 16, 32):
            sums[2 * reach] = sums[reach] + pltpu.roll(sums[reach], wide - reach, 1)
        total = sums[64] + pltpu.roll(sums[32], wide - 64, 1) + pltpu.roll(sums[4], wide - 96, 1)
        esum_ref[j] = total[:, :slab]


def window(power):
    blocks, piece, wide = power.shape
    return pl.pallas_call(
        window_kernel,
        in_specs=[VMEM],
        out_specs=VMEM,
        out_shape=jax.ShapeDtypeStruct((blocks, piece, wide - EDGE - 128), jnp.float32),
    )(power)


def finish_kernel(esum_ref, c_ref, n0_ref, n1_ref, n2_ref, out_ref):
    slab = out_ref.shape[2]
    for j, n_ref in enumerate((n0_ref, n1_ref, n2_ref)):
        count = c_ref[j, :, :1]
        norm = n_ref[:, slab + 64:slab + 65]
        scale = jnp.sqrt(count * TLEN)
        out_ref[j] = n_ref[:, :slab] * scale * lax.rsqrt(esum_ref[j] * norm + EPSILON)


def finish(esum, counts, n0, n1, n2):
    return pl.pallas_call(
        finish_kernel,
        in_specs=[VMEM] * 5,
        out_specs=VMEM,
        out_shape=jax.ShapeDtypeStruct(esum.shape, jnp.float32),
    )(esum, counts, n0, n1, n2)


def moved(block, distance):
    n = lax.axis_size("tm")
    return lax.ppermute(block, "tm", [(i, (i + distance) % n) for i in range(n)])


def swapped(block, distance):
    n = lax.axis_size("chan")
    return lax.ppermute(block, "chan", [(i, i ^ distance) for i in range(n)])


def scattered(keep, give, axis):
    distance = 1
    while True:
        total = keep + swapped(give, distance)
        left = total.shape[axis]
        if left == 1:
            return lax.squeeze(total, (axis,))
        distance *= 2
        mine = (lax.axis_index("chan") // distance) % 2
        shape = total.shape
        total = total.reshape(shape[:axis] + (left // 2, 2) + shape[axis + 1:])
        keep = lax.dynamic_index_in_dim(total, mine, axis + 1, keepdims=False)
        give = lax.dynamic_index_in_dim(total, 1 - mine, axis + 1, keepdims=False)


def local(data, templates, valid):
    pieces = lax.axis_size("chan")
    n = lax.axis_size("tm")
    at = lax.axis_index("tm")
    head = lax.ppermute(data[:, :EDGE], "tm", [(i + 1, i) for i in range(n - 1)])
    marks = valid.astype(jnp.bfloat16)
    marks1 = moved(marks, -1)
    marks2 = moved(marks, -2)
    earlier = moved(data, 1)
    earliest = moved(data, 2)
    mine = lax.axis_index("chan") % 2
    flags1 = jnp.stack([mine, (at != 0).astype(jnp.int32)])
    flags2 = jnp.stack([mine, (at != 1).astype(jnp.int32)])
    w, keep, give, power_keep, power_give = first(flags1, templates, marks, marks1, marks2, data, head, pieces)
    power = scattered(power_keep, power_give, 1)
    num0 = scattered(keep, give, 0)
    num1 = scattered(*later(flags1, w, earlier, data, pieces), 0)
    num2 = scattered(*later(flags2, w, earliest, earlier, pieces), 0)
    counts = power[:, :, -128:]
    norm = counts[0]
    home1 = moved(jnp.concatenate([num1, norm], axis=1), -1)
    home2 = moved(jnp.concatenate([num2, norm], axis=1), -2)
    return finish(window(power), counts, jnp.concatenate([num0, norm], axis=1), home1, home2)


def solution(mesh):
    placed = (P("chan", "tm"), P("tm", "chan"), P("tm", "chan"))
    return jax.shard_map(
        local, mesh=mesh, in_specs=placed, out_specs=P(None, "chan", "tm"), check_vma=False
    )
```

```python
import jax
import jax.numpy as jnp
from jax import lax
from jax.experimental import pallas as pl
from jax.experimental.pallas import tpu as pltpu
from jax.sharding import PartitionSpec as P

TLEN = 100
EPSILON = 1e-06
SIDE = 16
STEP = 32
EDGE = 128
MIB = 1024 * 1024
PAIRS = (TLEN + 2) // 2
TAPS = 2 * PAIRS + 1

VMEM = pl.BlockSpec(memory_space=pltpu.VMEM)
ANY = pl.BlockSpec(memory_space=pl.ANY)
HBM = pl.BlockSpec(memory_space=pltpu.HBM)
F32, BF16 = jnp.float32, jnp.bfloat16


def relayout(t_hbm, t_ref, v_ref, w, tall, mask, arrived):
    chans = v_ref.shape[1]
    wide = STEP * TLEN
    mask[...] = v_ref[...].astype(F32).T
    blank = jnp.zeros(w.shape[1:], w.dtype)
    w[0] = blank
    for tap in range(TLEN + 1, TAPS):
        w[tap] = blank

    def step(i, total):
        columns = pl.ds(pl.multiple_of(i * wide, wide), wide)
        channels = pl.ds(pl.multiple_of(i * STEP, STEP), STEP)
        pltpu.make_async_copy(t_hbm.at[:, columns], t_ref.at[:, columns], arrived.at[i]).wait()
        tall[...] = t_ref[:, columns].T.astype(F32)
        keep = mask[channels, :]

        def tap(l, total):
            kernel = tall[pl.ds(l, STEP, stride=TLEN), :] * keep
            w[l + 1, channels, :] = kernel.astype(w.dtype)
            return total + kernel * kernel

        return lax.fori_loop(0, TLEN, tap, total, unroll=10)

    total = lax.fori_loop(0, chans // STEP, step, jnp.zeros((STEP, w.shape[2]), F32))
    norm = jnp.sum(total, axis=0, keepdims=True)
    return jnp.broadcast_to(norm, (128, norm.shape[1])).T


def interleave(x_ref, h_ref, turned, windows, edge, open_at):
    chans, slab = x_ref.shape
    lanes = turned.shape[2]
    step = slab // SIDE
    spans = [slice(at, min(at + lanes, chans)) for at in range(0, chans, lanes)]
    for b, rows in enumerate(spans):
        turned[b, :slab, :rows.stop - rows.start] = x_ref[rows, :].T.astype(F32)
    edge.wait()
    follows = jnp.float32(1) if open_at is None else (lax.axis_index("tm") != open_at).astype(F32)
    for b, rows in enumerate(spans):
        turned[b, slab:, :rows.stop - rows.start] = h_ref[rows, :].T.astype(F32) * follows
    for a in range(windows.shape[0] // SIDE):
        for p in range(2):
            for b, rows in enumerate(spans):
                n = rows.stop - rows.start
                samples = turned[b, pl.ds(2 * a + p, SIDE, stride=step), :]
                at = p * chans + rows.start
                windows[a * SIDE:(a + 1) * SIDE, at:at + n] = samples[:, :n].astype(windows.dtype)


def correlate(w, windows, acc, flat):
    half, rows = acc.shape[1:]
    left = [windows[q * SIDE:q * SIDE + half, :] for q in range(PAIRS)]
    right = [jnp.concatenate([w[m + 1], w[m]], axis=1) for m in range(2 * PAIRS)]
    d = jnp.dot(jnp.concatenate(left, axis=1), jnp.concatenate(right, axis=0), preferred_element_type=F32)
    for r in range(2):
        acc[r] = d[:, r * rows:(r + 1) * rows]
    inner = half // SIDE
    for r in range(2):
        for b in range(SIDE):
            flat[pl.ds(2 * inner * b + r, inner, stride=2), :] = acc[r, pl.ds(b, inner, stride=SIDE), :]


def hand_out(rows_of, keep_ref, give_ref):
    mine = lax.axis_index("chan")
    piece = keep_ref.shape[-2]
    for d in range(2 * keep_ref.shape[0]):
        block = rows_of(pl.ds(pl.multiple_of((mine ^ d) * piece, piece), piece))
        (give_ref if d % 2 else keep_ref)[d // 2] = block


def traces(flat, norm, whole, keep_ref, give_ref):
    slab = flat.shape[0]
    whole[:, :slab] = flat[...].T
    whole[:, slab:] = norm
    hand_out(lambda rows: whole[rows, :], keep_ref, give_ref)


def power_kernel(x_hbm, h_ref, v_hbm, v1_ref, v2_ref, keep_ref, give_ref, x_ref, v0_ref, sems):
    copies = [pltpu.make_async_copy(v_hbm, v0_ref, sems.at[0]), pltpu.make_async_copy(x_hbm, x_ref, sems.at[1])]
    for copy in copies:
        copy.start()
    for copy in copies:
        copy.wait()
    slab = x_ref.shape[1]
    pieces, blocks, piece, wide = keep_ref.shape
    pieces *= 2
    mine = lax.axis_index("chan")
    valid = jnp.concatenate([
        r[pl.ds(pl.multiple_of((mine ^ d) * piece, piece), piece), :].astype(F32)
        for d in range(pieces) for r in (v0_ref, v1_ref, v2_ref)
    ], axis=0)
    count = jnp.sum(valid, axis=1, keepdims=True)
    valid = valid.astype(BF16)
    for at in range(0, wide, 128):
        part = x_ref[:, at:at + 128] if at < slab else h_ref[:, at - slab:at - slab + 128]
        square = jnp.square(part.astype(F32))
        high = square.astype(BF16)
        low = (square - high.astype(F32)).astype(BF16)
        total = jnp.dot(valid, high, preferred_element_type=F32) + jnp.dot(valid, low, preferred_element_type=F32)
        if at + 128 == wide:
            lane = lax.broadcasted_iota(jnp.int32, total.shape, 1)
            total = jnp.where(lane == 127, count, total)
        total = total.reshape(pieces, blocks, piece, 128)
        for d in range(pieces):
            (give_ref if d % 2 else keep_ref)[d // 2, :, :, at:at + 128] = total[d]


def relayout_kernel(t_hbm, v_hbm, w, norm_ref, t_ref, v_ref, tall, mask, arrived, sem):
    copy = pltpu.make_async_copy(v_hbm, v_ref, sem)
    copy.start()
    wide = STEP * TLEN
    for i in range(v_ref.shape[1] // STEP):
        columns = pl.ds(i * wide, wide)
        pltpu.make_async_copy(t_hbm.at[:, columns], t_ref.at[:, columns], arrived.at[i]).start()
    copy.wait()
    norm_ref[...] = relayout(t_hbm, t_ref, v_ref, w, tall, mask, arrived)


def slab_kernel(open_at, w, norm_ref, x_ref, next_hbm, keep_ref, give_ref, h_ref, turned, windows, acc, flat, whole, arrived):
    edge = pltpu.make_async_copy(next_hbm.at[:, pl.ds(0, EDGE)], h_ref, arrived)
    edge.start()
    interleave(x_ref, h_ref, turned, windows, edge, open_at)
    correlate(w, windows, acc, flat)
    traces(flat, norm_ref[...], whole, keep_ref, give_ref)


def scratch(chans, slab, rows):
    half = slab // 2
    return [
        pltpu.VMEM((-(-chans // 128), slab + EDGE, 128), F32),
        pltpu.VMEM((half + (PAIRS - 1) * SIDE, 2 * chans), BF16),
        pltpu.VMEM((2, half, rows), F32),
        pltpu.VMEM((slab, rows), F32),
        pltpu.VMEM((rows, slab + 128), F32),
    ]


def edge_kernel(x_hbm, out_ref, sem):
    copy = pltpu.make_async_copy(x_hbm.at[:, pl.ds(0, EDGE)], out_ref, sem)
    copy.start()
    copy.wait()


def edge_of(x):
    chans = x.shape[0]
    return pl.pallas_call(
        edge_kernel,
        in_specs=[HBM],
        out_specs=VMEM,
        out_shape=jax.ShapeDtypeStruct((chans, EDGE), x.dtype),
        scratch_shapes=[pltpu.SemaphoreType.DMA],
        compiler_params=pltpu.CompilerParams(vmem_limit_bytes=MIB),
        cost_estimate=pl.CostEstimate(flops=chans * 2 ** 26, bytes_accessed=4 * chans * EDGE, transcendentals=0),
    )(x)


def power_of(x, h, valids, pieces):
    chans, slab = x.shape
    rows = valids[0].shape[0]
    return pl.pallas_call(
        power_kernel,
        in_specs=[HBM, VMEM, HBM, VMEM, VMEM],
        out_specs=[VMEM] * 2,
        out_shape=[jax.ShapeDtypeStruct((pieces // 2, 3, rows // pieces, slab + EDGE), F32)] * 2,
        scratch_shapes=[pltpu.VMEM(x.shape, x.dtype), pltpu.VMEM(valids[0].shape, jnp.int32), pltpu.SemaphoreType.DMA((2,))],
        compiler_params=pltpu.CompilerParams(vmem_limit_bytes=12 * MIB),
        cost_estimate=pl.CostEstimate(flops=12 * rows * chans * slab, bytes_accessed=16 * rows * slab, transcendentals=0),
    )(x, h, *valids)


def tap_major(templates, valid):
    rows, chans = valid.shape
    return pl.pallas_call(
        relayout_kernel,
        in_specs=[HBM] * 2,
        out_specs=[VMEM] * 2,
        out_shape=[jax.ShapeDtypeStruct((TAPS, chans, rows), BF16), jax.ShapeDtypeStruct((rows, 128), F32)],
        scratch_shapes=[
            pltpu.VMEM(templates.shape, templates.dtype),
            pltpu.VMEM(valid.shape, valid.dtype),
            pltpu.VMEM((STEP * TLEN, rows), F32),
            pltpu.VMEM((chans, rows), F32),
            pltpu.SemaphoreType.DMA((chans // STEP,)),
            pltpu.SemaphoreType.DMA,
        ],
        compiler_params=pltpu.CompilerParams(vmem_limit_bytes=26 * MIB),
        cost_estimate=pl.CostEstimate(flops=0, bytes_accessed=4 * rows * chans * TLEN, transcendentals=0),
    )(templates, valid)


def correlated(w, norm, x, follows, open_at, pieces):
    chans, slab = x.shape
    rows = w.shape[2]
    return pl.pallas_call(
        lambda *refs: slab_kernel(open_at, *refs),
        in_specs=[VMEM, VMEM, VMEM, ANY],
        out_specs=[VMEM] * 2,
        out_shape=[jax.ShapeDtypeStruct((pieces // 2, rows // pieces, slab + 128), F32)] * 2,
        scratch_shapes=[pltpu.VMEM((chans, EDGE), x.dtype)] + scratch(chans, slab, rows) + [pltpu.SemaphoreType.DMA],
        compiler_params=pltpu.CompilerParams(vmem_limit_bytes=18 * MIB),
        cost_estimate=pl.CostEstimate(flops=3 * rows * chans * TLEN * slab, bytes_accessed=2 * rows * chans * TLEN, transcendentals=0),
    )(w, norm, x, follows)


def added(refs):
    total = refs[0][...]
    for ref in refs[1:]:
        total = total + ref[...]
    return total


def windowed(power, wide):
    sums = {1: power}
    for reach in (1, 2, 4, 8, 16, 32):
        sums[2 * reach] = sums[reach] + pltpu.roll(sums[reach], wide - reach, 1)
    return sums[64] + pltpu.roll(sums[32], wide - 64, 1) + pltpu.roll(sums[4], wide - 96, 1)


def scaled(num, esum, count):
    slab = esum.shape[1]
    norm = num[:, slab:slab + 1]
    return num[:, :slab] * jnp.sqrt(count * TLEN) * lax.rsqrt(esum * norm + EPSILON)


def early_kernel(parts, *refs):
    powers, num0, num1 = refs[:parts], refs[parts:2 * parts], refs[2 * parts:-3]
    out_ref, esum_ref, count_ref = refs[-3:]
    slab = out_ref.shape[2]
    wide = slab + EDGE
    num0 = [r.at[0] for r in num0[:2]] + list(num0[2:])
    for j in range(3):
        power = added([r.at[0, j] for r in powers[:2]] + [r.at[j] for r in powers[2:]])
        esum = windowed(power, wide)[:, :slab]
        count = power[:, wide - 1:]
        if j < 2:
            out_ref[j] = scaled(added((num0, num1)[j]), esum, count)
        else:
            esum_ref[...] = esum
            count_ref[...] = jnp.broadcast_to(count, count_ref.shape)


def early(powers, num0, num1):
    piece, wide = num1[0].shape
    slab = wide - 128
    parts = len(powers)
    return pl.pallas_call(
        lambda *refs: early_kernel(parts, *refs),
        in_specs=[VMEM] * (2 * parts + len(num1)),
        out_specs=[VMEM] * 3,
        out_shape=[jax.ShapeDtypeStruct((3, piece, slab), F32), jax.ShapeDtypeStruct((piece, slab), F32), jax.ShapeDtypeStruct((piece, 128), F32)],
        compiler_params=pltpu.CompilerParams(vmem_limit_bytes=12 * MIB),
    )(*powers, *num0, *num1)


def last_kernel(pieces, _, esum_ref, count_ref, *refs):
    parts, out_hbm, trace, sent = refs[:pieces], refs[pieces], refs[pieces + 1], refs[pieces + 2]
    trace[...] = scaled(added(parts), esum_ref[...], count_ref[:, :1])
    copy = pltpu.make_async_copy(trace, out_hbm.at[2], sent)
    copy.start()
    copy.wait()


def last(out, esum, count, parts):
    return pl.pallas_call(
        lambda *refs: last_kernel(len(parts), *refs),
        in_specs=[ANY] + [VMEM] * (2 + len(parts)),
        out_specs=ANY,
        out_shape=jax.ShapeDtypeStruct(out.shape, out.dtype),
        scratch_shapes=[pltpu.VMEM(esum.shape, F32), pltpu.SemaphoreType.DMA],
        input_output_aliases={0: 0},
        compiler_params=pltpu.CompilerParams(vmem_limit_bytes=4 * MIB),
    )(out, esum, count, *parts)


def sent(block, slabs, distance):
    n, m = lax.axis_size("tm"), lax.axis_size("chan")
    if distance == 0:
        return lax.ppermute(block, "tm", [(i, (i + slabs) % n) for i in range(n)]) if slabs else block
    if slabs == 0:
        return lax.ppermute(block, "chan", [(k, k ^ distance) for k in range(m)])
    route = [(i * m + k, (i + slabs) % n * m + (k ^ distance)) for i in range(n) for k in range(m)]
    return lax.ppermute(block, ("tm", "chan"), route)


together = lax.optimization_barrier


def local(data, templates, valid):
    pieces = lax.axis_size("chan")
    n = lax.axis_size("tm")
    others = range(1, pieces // 2)
    head = lax.ppermute(edge_of(data), "tm", [(i + 1, i) for i in range(n - 1)])
    valid1 = sent(valid, -1, 0)
    valid2 = sent(valid, -2, 0)
    w, norm = tap_major(templates, valid)
    w, head, valid1, valid2, moving = together((w, head, valid1, valid2, data))
    earlier = sent(moving, 1, 0)
    earliest = sent(moving, 2, 0)

    power_keep, power_give = power_of(data, head, (valid, valid1, valid2), pieces)
    head, power_give = together((head, power_give))
    power_got = sent(power_give, 0, 1)

    keep0, give0 = correlated(w, norm, data, head, None, pieces)
    give0, power_got = together((give0, power_got))
    got0 = sent(give0, 0, 1)
    powers = [power_keep[d] + power_got[d] for d in others]
    earlier, powers = together((earlier, powers))
    powers = [sent(part, 0, 2 * d) for d, part in zip(others, powers)]

    keep1, give1 = correlated(w, norm, earlier, data, 0, pieces)
    give1, got0, powers = together((give1, got0, powers))
    got1 = sent(give1, 0, 1)
    num0 = [keep0[d] + got0[d] for d in others]
    num1 = [keep1[d] + got1[d] for d in range(pieces // 2)]
    earliest, num0, num1 = together((earliest, num0, num1))
    num0 = [sent(part, 0, 2 * d) for d, part in zip(others, num0)]
    num1 = [sent(part, -1, 2 * d) for d, part in enumerate(num1)]

    keep2, give2 = correlated(w, norm, earliest, earlier, 1, pieces)
    give2, num1, num0 = together((give2, num1, num0))
    got2 = sent(give2, 0, 1)
    num2 = [keep2[d] + got2[d] for d in range(pieces // 2)]
    num2 = [sent(part, -2, 2 * d) for d, part in enumerate(num2)]
    out, esum, count = early([power_keep, power_got] + powers, [keep0, got0] + num0, num1)
    return last(out, esum, count, num2)


def solution(mesh):
    placed = (P("chan", "tm"), P("tm", "chan"), P("tm", "chan"))
    return jax.shard_map(
        local, mesh=mesh, in_specs=placed, out_specs=P(None, "chan", "tm"), check_vma=False
    )
```

```python
import jax
import jax.numpy as jnp
from jax import lax
from jax.experimental import pallas as pl
from jax.experimental.pallas import tpu as pltpu
from jax.sharding import PartitionSpec as P

TLEN = 100
EPSILON = 1e-06
SIDE = 16
STEP = 64
EDGE = 128
MIB = 1024 * 1024
PAIRS = (TLEN + 2) // 2
TAPS = 2 * PAIRS + 1

VMEM = pl.BlockSpec(memory_space=pltpu.VMEM)
ANY = pl.BlockSpec(memory_space=pl.ANY)
HBM = pl.BlockSpec(memory_space=pltpu.HBM)
F32, BF16 = jnp.float32, jnp.bfloat16


def relayout(t_ref, v_ref, w, tall, mask):
    chans = v_ref.shape[1]
    wide = STEP * TLEN
    mask[...] = v_ref[...].astype(F32).T
    blank = jnp.zeros(w.shape[1:], w.dtype)
    w[0] = blank
    for tap in range(TLEN + 1, TAPS):
        w[tap] = blank

    def step(i, total):
        columns = pl.ds(pl.multiple_of(i * wide, wide), wide)
        channels = pl.ds(pl.multiple_of(i * STEP, STEP), STEP)
        tall[...] = t_ref[:, columns].T.astype(F32)
        keep = mask[channels, :]

        def tap(l, total):
            kernel = tall[pl.ds(l, STEP, stride=TLEN), :] * keep
            w[l + 1, channels, :] = kernel.astype(w.dtype)
            return total + kernel * kernel

        return lax.fori_loop(0, TLEN, tap, total, unroll=50)

    total = lax.fori_loop(0, chans // STEP, step, jnp.zeros((STEP, w.shape[2]), F32))
    norm = jnp.sum(total, axis=0, keepdims=True)
    return jnp.broadcast_to(norm, (128, norm.shape[1])).T


def interleave(x_ref, next_ref, turned, windows, open_at):
    chans, slab = x_ref.shape
    lanes = turned.shape[2]
    step = slab // SIDE
    spans = [slice(at, min(at + lanes, chans)) for at in range(0, chans, lanes)]
    for b, rows in enumerate(spans):
        turned[b, :slab, :rows.stop - rows.start] = x_ref[rows, :].T.astype(F32)
    follows = jnp.float32(1) if open_at is None else (lax.axis_index("tm") != open_at).astype(F32)
    for b, rows in enumerate(spans):
        turned[b, slab:, :rows.stop - rows.start] = next_ref[rows, :EDGE].T.astype(F32) * follows
    for a in range(windows.shape[0] // SIDE):
        for p in range(2):
            for b, rows in enumerate(spans):
                n = rows.stop - rows.start
                samples = turned[b, pl.ds(2 * a + p, SIDE, stride=step), :]
                at = p * chans + rows.start
                windows[a * SIDE:(a + 1) * SIDE, at:at + n] = samples[:, :n].astype(windows.dtype)


def correlate(w, windows, acc, flat):
    half, rows = acc.shape[1:]
    left = [windows[q * SIDE:q * SIDE + half, :] for q in range(PAIRS)]
    right = [jnp.concatenate([w[m + 1], w[m]], axis=1) for m in range(2 * PAIRS)]
    d = jnp.dot(jnp.concatenate(left, axis=1), jnp.concatenate(right, axis=0), preferred_element_type=F32)
    for r in range(2):
        acc[r] = d[:, r * rows:(r + 1) * rows]
    inner = half // SIDE
    for r in range(2):
        for b in range(SIDE):
            flat[pl.ds(2 * inner * b + r, inner, stride=2), :] = acc[r, pl.ds(b, inner, stride=SIDE), :]


def hand_out(rows_of, keep_ref, give_ref):
    mine = lax.axis_index("chan")
    piece = keep_ref.shape[-2]
    for d in range(2 * keep_ref.shape[0]):
        block = rows_of(pl.ds(pl.multiple_of((mine ^ d) * piece, piece), piece))
        (give_ref if d % 2 else keep_ref)[d // 2] = block


def traces(flat, norm, whole, keep_ref, give_ref):
    slab = flat.shape[0]
    whole[:, :slab] = flat[...].T
    whole[:, slab:] = norm
    hand_out(lambda rows: whole[rows, :], keep_ref, give_ref)


def power_kernel(x_ref, h_ref, v0_ref, v1_ref, v2_ref, keep_ref, give_ref):
    slab = x_ref.shape[1]
    pieces, blocks, piece, wide = keep_ref.shape
    pieces *= 2
    mine = lax.axis_index("chan")
    valid = jnp.concatenate([
        r[pl.ds(pl.multiple_of((mine ^ d) * piece, piece), piece), :].astype(F32)
        for d in range(pieces) for r in (v0_ref, v1_ref, v2_ref)
    ], axis=0)
    count = jnp.sum(valid, axis=1, keepdims=True)
    valid = valid.astype(BF16)
    for at in range(0, wide, 128):
        part = x_ref[:, at:at + 128] if at < slab else h_ref[:, at - slab:at - slab + 128]
        square = jnp.square(part.astype(F32))
        high = square.astype(BF16)
        low = (square - high.astype(F32)).astype(BF16)
        total = jnp.dot(valid, high, preferred_element_type=F32) + jnp.dot(valid, low, preferred_element_type=F32)
        if at + 128 == wide:
            lane = lax.broadcasted_iota(jnp.int32, total.shape, 1)
            total = jnp.where(lane == 127, count, total)
        total = total.reshape(pieces, blocks, piece, 128)
        for d in range(pieces):
            (give_ref if d % 2 else keep_ref)[d // 2, :, :, at:at + 128] = total[d]


def relayout_kernel(t_ref, v_ref, w, norm_ref, tall, mask):
    norm_ref[...] = relayout(t_ref, v_ref, w, tall, mask)


def slab_kernel(open_at, w, norm_ref, x_ref, next_ref, keep_ref, give_ref, turned, windows, acc, flat, whole):
    interleave(x_ref, next_ref, turned, windows, open_at)
    correlate(w, windows, acc, flat)
    traces(flat, norm_ref[...], whole, keep_ref, give_ref)


def scratch(chans, slab, rows):
    half = slab // 2
    return [
        pltpu.VMEM((-(-chans // 128), slab + EDGE, 128), F32),
        pltpu.VMEM((half + (PAIRS - 1) * SIDE, 2 * chans), BF16),
        pltpu.VMEM((2, half, rows), F32),
        pltpu.VMEM((slab, rows), F32),
        pltpu.VMEM((rows, slab + 128), F32),
    ]


def edge_kernel(x_hbm, out_ref, sem):
    copy = pltpu.make_async_copy(x_hbm.at[:, pl.ds(0, EDGE)], out_ref, sem)
    copy.start()
    copy.wait()


def edge_of(x):
    chans = x.shape[0]
    return pl.pallas_call(
        edge_kernel,
        in_specs=[HBM],
        out_specs=VMEM,
        out_shape=jax.ShapeDtypeStruct((chans, EDGE), x.dtype),
        scratch_shapes=[pltpu.SemaphoreType.DMA],
        compiler_params=pltpu.CompilerParams(vmem_limit_bytes=MIB),
        cost_estimate=pl.CostEstimate(flops=chans * 2 ** 26, bytes_accessed=4 * chans * EDGE, transcendentals=0),
    )(x)


def power_of(x, h, valids, pieces):
    chans, slab = x.shape
    rows = valids[0].shape[0]
    return pl.pallas_call(
        power_kernel,
        in_specs=[VMEM] * 5,
        out_specs=[VMEM] * 2,
        out_shape=[jax.ShapeDtypeStruct((pieces // 2, 3, rows // pieces, slab + EDGE), F32)] * 2,
        compiler_params=pltpu.CompilerParams(vmem_limit_bytes=12 * MIB),
        cost_estimate=pl.CostEstimate(flops=12 * rows * chans * slab, bytes_accessed=16 * rows * slab, transcendentals=0),
    )(x, h, *valids)


def tap_major(templates, valid):
    rows, chans = valid.shape
    return pl.pallas_call(
        relayout_kernel,
        in_specs=[VMEM] * 2,
        out_specs=[VMEM] * 2,
        out_shape=[jax.ShapeDtypeStruct((TAPS, chans, rows), BF16), jax.ShapeDtypeStruct((rows, 128), F32)],
        scratch_shapes=[pltpu.VMEM((STEP * TLEN, rows), F32), pltpu.VMEM((chans, rows), F32)],
        compiler_params=pltpu.CompilerParams(vmem_limit_bytes=26 * MIB),
        cost_estimate=pl.CostEstimate(flops=0, bytes_accessed=4 * rows * chans * TLEN, transcendentals=0),
    )(templates, valid)


def correlated(w, norm, x, follows, open_at, pieces):
    chans, slab = x.shape
    rows = w.shape[2]
    return pl.pallas_call(
        lambda *refs: slab_kernel(open_at, *refs),
        in_specs=[VMEM] * 4,
        out_specs=[VMEM] * 2,
        out_shape=[jax.ShapeDtypeStruct((pieces // 2, rows // pieces, slab + 128), F32)] * 2,
        scratch_shapes=scratch(chans, slab, rows),
        compiler_params=pltpu.CompilerParams(vmem_limit_bytes=18 * MIB),
        cost_estimate=pl.CostEstimate(flops=3 * rows * chans * TLEN * slab, bytes_accessed=2 * rows * chans * TLEN, transcendentals=0),
    )(w, norm, x, follows)


def added(refs):
    total = refs[0][...]
    for ref in refs[1:]:
        total = total + ref[...]
    return total


def windowed(power, wide):
    sums = {1: power}
    for reach in (1, 2, 4, 8, 16, 32):
        sums[2 * reach] = sums[reach] + pltpu.roll(sums[reach], wide - reach, 1)
    return sums[64] + pltpu.roll(sums[32], wide - 64, 1) + pltpu.roll(sums[4], wide - 96, 1)


def scaled(num, esum, count):
    slab = esum.shape[1]
    norm = num[:, slab:slab + 1]
    return num[:, :slab] * jnp.sqrt(count * TLEN) * lax.rsqrt(esum * norm + EPSILON)


def early_kernel(parts, *refs):
    powers, num0, num1 = refs[:parts], refs[parts:2 * parts], refs[2 * parts:-3]
    out_ref, esum_ref, count_ref = refs[-3:]
    slab = out_ref.shape[2]
    wide = slab + EDGE
    num0 = [r.at[0] for r in num0[:2]] + list(num0[2:])
    for j in range(3):
        power = added([r.at[0, j] for r in powers[:2]] + [r.at[j] for r in powers[2:]])
        esum = windowed(power, wide)[:, :slab]
        count = power[:, wide - 1:]
        if j < 2:
            out_ref[j] = scaled(added((num0, num1)[j]), esum, count)
        else:
            esum_ref[...] = esum
            count_ref[...] = jnp.broadcast_to(count, count_ref.shape)


def early(powers, num0, num1):
    piece, wide = num1[0].shape
    slab = wide - 128
    parts = len(powers)
    return pl.pallas_call(
        lambda *refs: early_kernel(parts, *refs),
        in_specs=[VMEM] * (2 * parts + len(num1)),
        out_specs=[VMEM] * 3,
        out_shape=[jax.ShapeDtypeStruct((3, piece, slab), F32), jax.ShapeDtypeStruct((piece, slab), F32), jax.ShapeDtypeStruct((piece, 128), F32)],
        compiler_params=pltpu.CompilerParams(vmem_limit_bytes=12 * MIB),
    )(*powers, *num0, *num1)


def last_kernel(pieces, _, esum_ref, count_ref, *refs):
    parts, out_hbm, trace, sent = refs[:pieces], refs[pieces], refs[pieces + 1], refs[pieces + 2]
    trace[...] = scaled(added(parts), esum_ref[...], count_ref[:, :1])
    copy = pltpu.make_async_copy(trace, out_hbm.at[2], sent)
    copy.start()
    copy.wait()


def last(out, esum, count, parts):
    return pl.pallas_call(
        lambda *refs: last_kernel(len(parts), *refs),
        in_specs=[ANY] + [VMEM] * (2 + len(parts)),
        out_specs=ANY,
        out_shape=jax.ShapeDtypeStruct(out.shape, out.dtype),
        scratch_shapes=[pltpu.VMEM(esum.shape, F32), pltpu.SemaphoreType.DMA],
        input_output_aliases={0: 0},
        compiler_params=pltpu.CompilerParams(vmem_limit_bytes=4 * MIB),
    )(out, esum, count, *parts)


def sent(block, slabs, distance):
    n, m = lax.axis_size("tm"), lax.axis_size("chan")
    if distance == 0:
        return lax.ppermute(block, "tm", [(i, (i + slabs) % n) for i in range(n)]) if slabs else block
    if slabs == 0:
        return lax.ppermute(block, "chan", [(k, k ^ distance) for k in range(m)])
    route = [(i * m + k, (i + slabs) % n * m + (k ^ distance)) for i in range(n) for k in range(m)]
    return lax.ppermute(block, ("tm", "chan"), route)


together = lax.optimization_barrier


def local(data, templates, valid):
    pieces = lax.axis_size("chan")
    n = lax.axis_size("tm")
    others = range(1, pieces // 2)
    head = lax.ppermute(edge_of(data), "tm", [(i + 1, i) for i in range(n - 1)])
    valid1 = sent(valid, -1, 0)
    valid2 = sent(valid, -2, 0)
    w, norm = tap_major(templates, valid)
    w, head, valid1, valid2, moving = together((w, head, valid1, valid2, data))
    earlier = sent(moving, 1, 0)
    earliest = sent(moving, 2, 0)

    power_keep, power_give = power_of(data, head, (valid, valid1, valid2), pieces)
    head, power_give = together((head, power_give))
    power_got = sent(power_give, 0, 1)

    keep0, give0 = correlated(w, norm, data, head, None, pieces)
    give0, power_got = together((give0, power_got))
    got0 = sent(give0, 0, 1)
    powers = [power_keep[d] + power_got[d] for d in others]
    earlier, powers = together((earlier, powers))
    powers = [sent(part, 0, 2 * d) for d, part in zip(others, powers)]

    keep1, give1 = correlated(w, norm, earlier, data, 0, pieces)
    give1, got0, powers = together((give1, got0, powers))
    got1 = sent(give1, 0, 1)
    num0 = [keep0[d] + got0[d] for d in others]
    num1 = [keep1[d] + got1[d] for d in range(pieces // 2)]
    earliest, num0, num1 = together((earliest, num0, num1))
    num0 = [sent(part, 0, 2 * d) for d, part in zip(others, num0)]
    num1 = [sent(part, -1, 2 * d) for d, part in enumerate(num1)]

    keep2, give2 = correlated(w, norm, earliest, earlier, 1, pieces)
    give2, num1, num0 = together((give2, num1, num0))
    got2 = sent(give2, 0, 1)
    num2 = [keep2[d] + got2[d] for d in range(pieces // 2)]
    num2 = [sent(part, -2, 2 * d) for d, part in enumerate(num2)]
    out, esum, count = early([power_keep, power_got] + powers, [keep0, got0] + num0, num1)
    return last(out, esum, count, num2)


def solution(mesh):
    placed = (P("chan", "tm"), P("tm", "chan"), P("tm", "chan"))
    return jax.shard_map(
        local, mesh=mesh, in_specs=placed, out_specs=P(None, "chan", "tm"), check_vma=False
    )
```

```python
import jax
import jax.numpy as jnp
from jax import lax
from jax.experimental import pallas as pl
from jax.experimental.pallas import tpu as pltpu
from jax.sharding import PartitionSpec as P

TLEN = 100
EPSILON = 1e-06
SIDE = 16
STEP = 64
EDGE = 128
MIB = 1024 * 1024
PAIRS = (TLEN + 2) // 2
TAPS = 2 * PAIRS + 1

VMEM = pl.BlockSpec(memory_space=pltpu.VMEM)
ANY = pl.BlockSpec(memory_space=pl.ANY)
HBM = pl.BlockSpec(memory_space=pltpu.HBM)
F32, BF16 = jnp.float32, jnp.bfloat16


def relayout(t_ref, v_ref, w, tall, mask):
    chans = v_ref.shape[1]
    wide = STEP * TLEN
    mask[...] = v_ref[...].astype(F32).T
    blank = jnp.zeros(w.shape[1:], w.dtype)
    w[0] = blank
    for tap in range(TLEN + 1, TAPS):
        w[tap] = blank

    def step(i, total):
        columns = pl.ds(pl.multiple_of(i * wide, wide), wide)
        channels = pl.ds(pl.multiple_of(i * STEP, STEP), STEP)
        tall[...] = t_ref[:, columns].T.astype(F32)
        keep = mask[channels, :]

        def tap(l, total):
            kernel = tall[pl.ds(l, STEP, stride=TLEN), :] * keep
            w[l + 1, channels, :] = kernel.astype(w.dtype)
            return total + kernel * kernel

        return lax.fori_loop(0, TLEN, tap, total, unroll=50)

    total = lax.fori_loop(0, chans // STEP, step, jnp.zeros((STEP, w.shape[2]), F32))
    norm = jnp.sum(total, axis=0, keepdims=True)
    return jnp.broadcast_to(norm, (128, norm.shape[1])).T


def interleave(x_ref, next_ref, turned, windows, open_at):
    chans, slab = x_ref.shape
    lanes = turned.shape[2]
    step = slab // SIDE
    spans = [slice(at, min(at + lanes, chans)) for at in range(0, chans, lanes)]
    for b, rows in enumerate(spans):
        turned[b, :slab, :rows.stop - rows.start] = x_ref[rows, :].T.astype(F32)
    follows = jnp.float32(1) if open_at is None else (lax.axis_index("tm") != open_at).astype(F32)
    for b, rows in enumerate(spans):
        turned[b, slab:, :rows.stop - rows.start] = next_ref[rows, :EDGE].T.astype(F32) * follows
    for a in range(windows.shape[0] // SIDE):
        for p in range(2):
            for b, rows in enumerate(spans):
                n = rows.stop - rows.start
                samples = turned[b, pl.ds(2 * a + p, SIDE, stride=step), :]
                at = p * chans + rows.start
                windows[a * SIDE:(a + 1) * SIDE, at:at + n] = samples[:, :n].astype(windows.dtype)


def correlate(w, windows, acc, flat):
    half, rows = acc.shape[1:]
    left = [windows[q * SIDE:q * SIDE + half, :] for q in range(PAIRS)]
    right = [jnp.concatenate([w[m + 1], w[m]], axis=1) for m in range(2 * PAIRS)]
    d = jnp.dot(jnp.concatenate(left, axis=1), jnp.concatenate(right, axis=0), preferred_element_type=F32)
    for r in range(2):
        acc[r] = d[:, r * rows:(r + 1) * rows]
    inner = half // SIDE
    for r in range(2):
        for b in range(SIDE):
            flat[pl.ds(2 * inner * b + r, inner, stride=2), :] = acc[r, pl.ds(b, inner, stride=SIDE), :]


def hand_out(rows_of, keep_ref, give_ref):
    mine = lax.axis_index("chan")
    piece = keep_ref.shape[-2]
    for d in range(2 * keep_ref.shape[0]):
        block = rows_of(pl.ds(pl.multiple_of((mine ^ d) * piece, piece), piece))
        (give_ref if d % 2 else keep_ref)[d // 2] = block


def traces(flat, norm, whole, keep_ref, give_ref):
    slab = flat.shape[0]
    whole[:, :slab] = flat[...].T
    whole[:, slab:] = norm
    hand_out(lambda rows: whole[rows, :], keep_ref, give_ref)


def power_kernel(x_ref, h_ref, v0_ref, v1_ref, v2_ref, keep_ref, give_ref):
    slab = x_ref.shape[1]
    pieces, blocks, piece, wide = keep_ref.shape
    pieces *= 2
    mine = lax.axis_index("chan")
    valid = jnp.concatenate([
        r[pl.ds(pl.multiple_of((mine ^ d) * piece, piece), piece), :].astype(F32)
        for d in range(pieces) for r in (v0_ref, v1_ref, v2_ref)
    ], axis=0)
    count = jnp.sum(valid, axis=1, keepdims=True)
    valid = valid.astype(BF16)
    for at in range(0, wide, 128):
        part = x_ref[:, at:at + 128] if at < slab else h_ref[:, at - slab:at - slab + 128]
        square = jnp.square(part.astype(F32))
        high = square.astype(BF16)
        low = (square - high.astype(F32)).astype(BF16)
        total = jnp.dot(valid, high, preferred_element_type=F32) + jnp.dot(valid, low, preferred_element_type=F32)
        if at + 128 == wide:
            lane = lax.broadcasted_iota(jnp.int32, total.shape, 1)
            total = jnp.where(lane == 127, count, total)
        total = total.reshape(pieces, blocks, piece, 128)
        for d in range(pieces):
            (give_ref if d % 2 else keep_ref)[d // 2, :, :, at:at + 128] = total[d]


def relayout_kernel(t_ref, v_ref, w, norm_ref, tall, mask):
    norm_ref[...] = relayout(t_ref, v_ref, w, tall, mask)


def slab_kernel(open_at, w, norm_ref, x_ref, next_ref, keep_ref, give_ref, turned, windows, acc, flat, whole):
    interleave(x_ref, next_ref, turned, windows, open_at)
    correlate(w, windows, acc, flat)
    traces(flat, norm_ref[...], whole, keep_ref, give_ref)


def scratch(chans, slab, rows):
    half = slab // 2
    return [
        pltpu.VMEM((-(-chans // 128), slab + EDGE, 128), F32),
        pltpu.VMEM((half + (PAIRS - 1) * SIDE, 2 * chans), BF16),
        pltpu.VMEM((2, half, rows), F32),
        pltpu.VMEM((slab, rows), F32),
        pltpu.VMEM((rows, slab + 128), F32),
    ]


def edge_kernel(x_hbm, out_ref, sem):
    copy = pltpu.make_async_copy(x_hbm.at[:, pl.ds(0, EDGE)], out_ref, sem)
    copy.start()
    copy.wait()


def edge_of(x):
    chans = x.shape[0]
    return pl.pallas_call(
        edge_kernel,
        in_specs=[HBM],
        out_specs=VMEM,
        out_shape=jax.ShapeDtypeStruct((chans, EDGE), x.dtype),
        scratch_shapes=[pltpu.SemaphoreType.DMA],
        compiler_params=pltpu.CompilerParams(vmem_limit_bytes=MIB),
        cost_estimate=pl.CostEstimate(flops=chans * 2 ** 26, bytes_accessed=4 * chans * EDGE, transcendentals=0),
    )(x)


def power_of(x, h, valids, pieces):
    chans, slab = x.shape
    rows = valids[0].shape[0]
    return pl.pallas_call(
        power_kernel,
        in_specs=[VMEM] * 5,
        out_specs=[VMEM] * 2,
        out_shape=[jax.ShapeDtypeStruct((pieces // 2, 3, rows // pieces, slab + EDGE), F32)] * 2,
        compiler_params=pltpu.CompilerParams(vmem_limit_bytes=12 * MIB),
        cost_estimate=pl.CostEstimate(flops=12 * rows * chans * slab, bytes_accessed=16 * rows * slab, transcendentals=0),
    )(x, h, *valids)


def tap_major(templates, valid):
    rows, chans = valid.shape
    return pl.pallas_call(
        relayout_kernel,
        in_specs=[VMEM] * 2,
        out_specs=[VMEM] * 2,
        out_shape=[jax.ShapeDtypeStruct((TAPS, chans, rows), BF16), jax.ShapeDtypeStruct((rows, 128), F32)],
        scratch_shapes=[pltpu.VMEM((STEP * TLEN, rows), F32), pltpu.VMEM((chans, rows), F32)],
        compiler_params=pltpu.CompilerParams(vmem_limit_bytes=26 * MIB),
        cost_estimate=pl.CostEstimate(flops=0, bytes_accessed=4 * rows * chans * TLEN, transcendentals=0),
    )(templates, valid)


def correlated(w, norm, x, follows, open_at, pieces):
    chans, slab = x.shape
    rows = w.shape[2]
    return pl.pallas_call(
        lambda *refs: slab_kernel(open_at, *refs),
        in_specs=[VMEM] * 4,
        out_specs=[VMEM] * 2,
        out_shape=[jax.ShapeDtypeStruct((pieces // 2, rows // pieces, slab + 128), F32)] * 2,
        scratch_shapes=scratch(chans, slab, rows),
        compiler_params=pltpu.CompilerParams(vmem_limit_bytes=18 * MIB),
        cost_estimate=pl.CostEstimate(flops=3 * rows * chans * TLEN * slab, bytes_accessed=2 * rows * chans * TLEN, transcendentals=0),
    )(w, norm, x, follows)


def added(refs):
    total = refs[0][...]
    for ref in refs[1:]:
        total = total + ref[...]
    return total


def windowed(power, wide):
    sums = {1: power}
    for reach in (1, 2, 4, 8, 16, 32):
        sums[2 * reach] = sums[reach] + pltpu.roll(sums[reach], wide - reach, 1)
    return sums[64] + pltpu.roll(sums[32], wide - 64, 1) + pltpu.roll(sums[4], wide - 96, 1)


def scaled(num, esum, count):
    slab = esum.shape[1]
    norm = num[:, slab:slab + 1]
    return num[:, :slab] * jnp.sqrt(count * TLEN) * lax.rsqrt(esum * norm + EPSILON)


def early_kernel(parts, *refs):
    powers, num0, num1 = refs[:parts], refs[parts:2 * parts], refs[2 * parts:-3]
    out_ref, esum_ref, count_ref = refs[-3:]
    slab = out_ref.shape[2]
    wide = slab + EDGE
    num0 = [r.at[0] for r in num0[:2]] + list(num0[2:])
    for j in range(3):
        power = added([r.at[0, j] for r in powers[:2]] + [r.at[j] for r in powers[2:]])
        esum = windowed(power, wide)[:, :slab]
        count = power[:, wide - 1:]
        if j < 2:
            out_ref[j] = scaled(added((num0, num1)[j]), esum, count)
        else:
            esum_ref[...] = esum
            count_ref[...] = jnp.broadcast_to(count, count_ref.shape)


def early(powers, num0, num1):
    piece, wide = num1[0].shape
    slab = wide - 128
    parts = len(powers)
    return pl.pallas_call(
        lambda *refs: early_kernel(parts, *refs),
        in_specs=[VMEM] * (2 * parts + len(num1)),
        out_specs=[VMEM] * 3,
        out_shape=[jax.ShapeDtypeStruct((3, piece, slab), F32), jax.ShapeDtypeStruct((piece, slab), F32), jax.ShapeDtypeStruct((piece, 128), F32)],
        compiler_params=pltpu.CompilerParams(vmem_limit_bytes=12 * MIB),
    )(*powers, *num0, *num1)


def last_kernel(pieces, _, esum_ref, count_ref, *refs):
    parts, out_hbm, trace, sent = refs[:pieces], refs[pieces], refs[pieces + 1], refs[pieces + 2]
    trace[...] = scaled(added(parts), esum_ref[...], count_ref[:, :1])
    copy = pltpu.make_async_copy(trace, out_hbm.at[2], sent)
    copy.start()
    copy.wait()


def last(out, esum, count, parts):
    return pl.pallas_call(
        lambda *refs: last_kernel(len(parts), *refs),
        in_specs=[ANY] + [VMEM] * (2 + len(parts)),
        out_specs=ANY,
        out_shape=jax.ShapeDtypeStruct(out.shape, out.dtype),
        scratch_shapes=[pltpu.VMEM(esum.shape, F32), pltpu.SemaphoreType.DMA],
        input_output_aliases={0: 0},
        compiler_params=pltpu.CompilerParams(vmem_limit_bytes=4 * MIB),
    )(out, esum, count, *parts)


def sent(block, slabs, distance):
    n, m = lax.axis_size("tm"), lax.axis_size("chan")
    if distance == 0:
        return lax.ppermute(block, "tm", [(i, (i + slabs) % n) for i in range(n)]) if slabs else block
    if slabs == 0:
        return lax.ppermute(block, "chan", [(k, k ^ distance) for k in range(m)])
    route = [(i * m + k, (i + slabs) % n * m + (k ^ distance)) for i in range(n) for k in range(m)]
    return lax.ppermute(block, ("tm", "chan"), route)


together = lax.optimization_barrier


def local(data, templates, valid):
    pieces = lax.axis_size("chan")
    n = lax.axis_size("tm")
    others = range(1, pieces // 2)
    head = lax.ppermute(edge_of(data), "tm", [(i + 1, i) for i in range(n - 1)])
    valid1 = sent(valid, -1, 0)
    valid2 = sent(valid, -2, 0)
    w, norm = tap_major(templates, valid)
    w, head, valid1, valid2, moving = together((w, head, valid1, valid2, data))
    earlier = sent(moving, 1, 0)
    earliest = sent(moving, 2, 0)

    power_keep, power_give = power_of(data, head, (valid, valid1, valid2), pieces)
    head, power_give = together((head, power_give))
    power_got = sent(power_give, 0, 1)

    keep0, give0 = correlated(w, norm, data, head, None, pieces)
    give0, power_got = together((give0, power_got))
    got0 = sent(give0, 0, 1)
    powers = [power_keep[d] + power_got[d] for d in others]
    earlier, _ = together((earlier, powers))
    powers = [sent(part, 0, 2 * d) for d, part in zip(others, powers)]

    keep1, give1 = correlated(w, norm, earlier, data, 0, pieces)
    give1, got0, powers = together((give1, got0, powers))
    got1 = sent(give1, 0, 1)
    num0 = [keep0[d] + got0[d] for d in others]
    num1 = [keep1[d] + got1[d] for d in range(pieces // 2)]
    earliest, _, _ = together((earliest, num0, num1))
    num0 = [sent(part, 0, 2 * d) for d, part in zip(others, num0)]
    num1 = [sent(part, -1, 2 * d) for d, part in enumerate(num1)]

    keep2, give2 = correlated(w, norm, earliest, earlier, 1, pieces)
    give2, num1, num0 = together((give2, num1, num0))
    got2 = sent(give2, 0, 1)
    num2 = [keep2[d] + got2[d] for d in range(pieces // 2)]
    num2 = [sent(part, -2, 2 * d) for d, part in enumerate(num2)]
    out, esum, count = early([power_keep, power_got] + powers, [keep0, got0] + num0, num1)
    return last(out, esum, count, num2)


def solution(mesh):
    placed = (P("chan", "tm"), P("tm", "chan"), P("tm", "chan"))
    return jax.shard_map(
        local, mesh=mesh, in_specs=placed, out_specs=P(None, "chan", "tm"), check_vma=False
    )
```

```python
import jax
import jax.numpy as jnp
from jax import lax
from jax.experimental import pallas as pl
from jax.experimental.pallas import tpu as pltpu
from jax.sharding import PartitionSpec as P

TLEN = 100
EPSILON = 1e-06
SIDE = 16
STEP = 64
EDGE = 128
MIB = 1024 * 1024
PAIRS = (TLEN + 2) // 2
TAPS = 2 * PAIRS + 1

VMEM = pl.BlockSpec(memory_space=pltpu.VMEM)
ANY = pl.BlockSpec(memory_space=pl.ANY)
HBM = pl.BlockSpec(memory_space=pltpu.HBM)
F32, BF16 = jnp.float32, jnp.bfloat16


def relayout(t_ref, v_ref, w, tall, mask):
    chans = v_ref.shape[1]
    wide = STEP * TLEN
    mask[...] = v_ref[...].astype(F32).T
    blank = jnp.zeros(w.shape[1:], w.dtype)
    w[0] = blank
    for tap in range(TLEN + 1, TAPS):
        w[tap] = blank

    def step(i, total):
        columns = pl.ds(pl.multiple_of(i * wide, wide), wide)
        channels = pl.ds(pl.multiple_of(i * STEP, STEP), STEP)
        tall[...] = t_ref[:, columns].T.astype(F32)
        keep = mask[channels, :]

        def tap(l, total):
            kernel = tall[pl.ds(l, STEP, stride=TLEN), :] * keep
            w[l + 1, channels, :] = kernel.astype(w.dtype)
            return total + kernel * kernel

        return lax.fori_loop(0, TLEN, tap, total, unroll=50)

    total = lax.fori_loop(0, chans // STEP, step, jnp.zeros((STEP, w.shape[2]), F32))
    norm = jnp.sum(total, axis=0, keepdims=True)
    return jnp.broadcast_to(norm, (128, norm.shape[1])).T


def interleave(x_ref, next_ref, turned, windows, open_at):
    chans, slab = x_ref.shape
    lanes = turned.shape[2]
    step = slab // SIDE
    spans = [slice(at, min(at + lanes, chans)) for at in range(0, chans, lanes)]
    for b, rows in enumerate(spans):
        turned[b, :slab, :rows.stop - rows.start] = x_ref[rows, :].T.astype(F32)
    follows = jnp.float32(1) if open_at is None else (lax.axis_index("tm") != open_at).astype(F32)
    for b, rows in enumerate(spans):
        turned[b, slab:, :rows.stop - rows.start] = next_ref[rows, :EDGE].T.astype(F32) * follows
    for a in range(windows.shape[0] // SIDE):
        for p in range(2):
            for b, rows in enumerate(spans):
                n = rows.stop - rows.start
                samples = turned[b, pl.ds(2 * a + p, SIDE, stride=step), :]
                at = p * chans + rows.start
                windows[a * SIDE:(a + 1) * SIDE, at:at + n] = samples[:, :n].astype(windows.dtype)


def correlate(w, windows, acc, flat):
    half, rows = acc.shape[1:]
    left = [windows[q * SIDE:q * SIDE + half, :] for q in range(PAIRS)]
    right = [jnp.concatenate([w[m + 1], w[m]], axis=1) for m in range(2 * PAIRS)]
    d = jnp.dot(jnp.concatenate(left, axis=1), jnp.concatenate(right, axis=0), preferred_element_type=F32)
    for r in range(2):
        acc[r] = d[:, r * rows:(r + 1) * rows]
    inner = half // SIDE
    for r in range(2):
        for b in range(SIDE):
            flat[pl.ds(2 * inner * b + r, inner, stride=2), :] = acc[r, pl.ds(b, inner, stride=SIDE), :]


def hand_out(rows_of, keep_ref, give_ref):
    mine = lax.axis_index("chan")
    piece = keep_ref.shape[-2]
    for d in range(2 * keep_ref.shape[0]):
        block = rows_of(pl.ds(pl.multiple_of((mine ^ d) * piece, piece), piece))
        (give_ref if d % 2 else keep_ref)[d // 2] = block


def traces(flat, norm, whole, keep_ref, give_ref):
    slab = flat.shape[0]
    whole[:, :slab] = flat[...].T
    whole[:, slab:] = norm
    hand_out(lambda rows: whole[rows, :], keep_ref, give_ref)


def power_kernel(x_ref, h_ref, v0_ref, v1_ref, v2_ref, keep_ref, give_ref):
    slab = x_ref.shape[1]
    pieces, blocks, piece, wide = keep_ref.shape
    pieces *= 2
    mine = lax.axis_index("chan")
    valid = jnp.concatenate([
        r[pl.ds(pl.multiple_of((mine ^ d) * piece, piece), piece), :].astype(F32)
        for d in range(pieces) for r in (v0_ref, v1_ref, v2_ref)
    ], axis=0)
    count = jnp.sum(valid, axis=1, keepdims=True)
    valid = valid.astype(BF16)
    for at in range(0, wide, 128):
        part = x_ref[:, at:at + 128] if at < slab else h_ref[:, at - slab:at - slab + 128]
        square = jnp.square(part.astype(F32))
        high = square.astype(BF16)
        low = (square - high.astype(F32)).astype(BF16)
        total = jnp.dot(valid, high, preferred_element_type=F32) + jnp.dot(valid, low, preferred_element_type=F32)
        if at + 128 == wide:
            lane = lax.broadcasted_iota(jnp.int32, total.shape, 1)
            total = jnp.where(lane == 127, count, total)
        total = total.reshape(pieces, blocks, piece, 128)
        for d in range(pieces):
            (give_ref if d % 2 else keep_ref)[d // 2, :, :, at:at + 128] = total[d]


def relayout_kernel(t_ref, v_ref, w, norm_ref, tall, mask):
    norm_ref[...] = relayout(t_ref, v_ref, w, tall, mask)


def slab_kernel(open_at, w, norm_ref, x_ref, next_ref, keep_ref, give_ref, turned, windows, acc, flat, whole):
    interleave(x_ref, next_ref, turned, windows, open_at)
    correlate(w, windows, acc, flat)
    traces(flat, norm_ref[...], whole, keep_ref, give_ref)


def scratch(chans, slab, rows):
    half = slab // 2
    return [
        pltpu.VMEM((-(-chans // 128), slab + EDGE, 128), F32),
        pltpu.VMEM((half + (PAIRS - 1) * SIDE, 2 * chans), BF16),
        pltpu.VMEM((2, half, rows), F32),
        pltpu.VMEM((slab, rows), F32),
        pltpu.VMEM((rows, slab + 128), F32),
    ]


def edge_kernel(x_hbm, out_ref, sem):
    copy = pltpu.make_async_copy(x_hbm.at[:, pl.ds(0, EDGE)], out_ref, sem)
    copy.start()
    copy.wait()


def edge_of(x):
    chans = x.shape[0]
    return pl.pallas_call(
        edge_kernel,
        in_specs=[HBM],
        out_specs=VMEM,
        out_shape=jax.ShapeDtypeStruct((chans, EDGE), x.dtype),
        scratch_shapes=[pltpu.SemaphoreType.DMA],
        compiler_params=pltpu.CompilerParams(vmem_limit_bytes=MIB),
        cost_estimate=pl.CostEstimate(flops=chans * 2 ** 26, bytes_accessed=4 * chans * EDGE, transcendentals=0),
    )(x)


def power_of(x, h, valids, pieces):
    chans, slab = x.shape
    rows = valids[0].shape[0]
    return pl.pallas_call(
        power_kernel,
        in_specs=[VMEM] * 5,
        out_specs=[VMEM] * 2,
        out_shape=[jax.ShapeDtypeStruct((pieces // 2, 3, rows // pieces, slab + EDGE), F32)] * 2,
        compiler_params=pltpu.CompilerParams(vmem_limit_bytes=12 * MIB),
        cost_estimate=pl.CostEstimate(flops=12 * rows * chans * slab, bytes_accessed=16 * rows * slab, transcendentals=0),
    )(x, h, *valids)


def tap_major(templates, valid):
    rows, chans = valid.shape
    return pl.pallas_call(
        relayout_kernel,
        in_specs=[VMEM] * 2,
        out_specs=[VMEM] * 2,
        out_shape=[jax.ShapeDtypeStruct((TAPS, chans, rows), BF16), jax.ShapeDtypeStruct((rows, 128), F32)],
        scratch_shapes=[pltpu.VMEM((STEP * TLEN, rows), F32), pltpu.VMEM((chans, rows), F32)],
        compiler_params=pltpu.CompilerParams(vmem_limit_bytes=26 * MIB),
        cost_estimate=pl.CostEstimate(flops=0, bytes_accessed=4 * rows * chans * TLEN, transcendentals=0),
    )(templates, valid)


def correlated(w, norm, x, follows, open_at, pieces):
    chans, slab = x.shape
    rows = w.shape[2]
    return pl.pallas_call(
        lambda *refs: slab_kernel(open_at, *refs),
        in_specs=[VMEM] * 4,
        out_specs=[VMEM] * 2,
        out_shape=[jax.ShapeDtypeStruct((pieces // 2, rows // pieces, slab + 128), F32)] * 2,
        scratch_shapes=scratch(chans, slab, rows),
        compiler_params=pltpu.CompilerParams(vmem_limit_bytes=18 * MIB),
        cost_estimate=pl.CostEstimate(flops=3 * rows * chans * TLEN * slab, bytes_accessed=2 * rows * chans * TLEN, transcendentals=0),
    )(w, norm, x, follows)


def added(refs):
    total = refs[0][...]
    for ref in refs[1:]:
        total = total + ref[...]
    return total


def windowed(power, wide):
    sums = {1: power}
    for reach in (1, 2, 4, 8, 16, 32):
        sums[2 * reach] = sums[reach] + pltpu.roll(sums[reach], wide - reach, 1)
    return sums[64] + pltpu.roll(sums[32], wide - 64, 1) + pltpu.roll(sums[4], wide - 96, 1)


def scaled(num, esum, count):
    slab = esum.shape[1]
    norm = num[:, slab:slab + 1]
    return num[:, :slab] * jnp.sqrt(count * TLEN) * lax.rsqrt(esum * norm + EPSILON)


def early_kernel(parts, *refs):
    powers, num0, num1 = refs[:parts], refs[parts:2 * parts], refs[2 * parts:-3]
    out_ref, esum_ref, count_ref = refs[-3:]
    slab = out_ref.shape[2]
    wide = slab + EDGE
    num0 = [r.at[0] for r in num0[:2]] + list(num0[2:])
    for j in range(3):
        power = added([r.at[0, j] for r in powers[:2]] + [r.at[j] for r in powers[2:]])
        esum = windowed(power, wide)[:, :slab]
        count = power[:, wide - 1:]
        if j < 2:
            out_ref[j] = scaled(added((num0, num1)[j]), esum, count)
        else:
            esum_ref[...] = esum
            count_ref[...] = jnp.broadcast_to(count, count_ref.shape)


def early(powers, num0, num1):
    piece, wide = num1[0].shape
    slab = wide - 128
    parts = len(powers)
    return pl.pallas_call(
        lambda *refs: early_kernel(parts, *refs),
        in_specs=[VMEM] * (2 * parts + len(num1)),
        out_specs=[VMEM] * 3,
        out_shape=[jax.ShapeDtypeStruct((3, piece, slab), F32), jax.ShapeDtypeStruct((piece, slab), F32), jax.ShapeDtypeStruct((piece, 128), F32)],
        compiler_params=pltpu.CompilerParams(vmem_limit_bytes=12 * MIB),
    )(*powers, *num0, *num1)


def last_kernel(pieces, _, esum_ref, count_ref, *refs):
    parts, out_hbm, trace, sent = refs[:pieces], refs[pieces], refs[pieces + 1], refs[pieces + 2]
    trace[...] = scaled(added(parts), esum_ref[...], count_ref[:, :1])
    copy = pltpu.make_async_copy(trace, out_hbm.at[2], sent)
    copy.start()
    copy.wait()


def last(out, esum, count, parts):
    return pl.pallas_call(
        lambda *refs: last_kernel(len(parts), *refs),
        in_specs=[ANY] + [VMEM] * (2 + len(parts)),
        out_specs=ANY,
        out_shape=jax.ShapeDtypeStruct(out.shape, out.dtype),
        scratch_shapes=[pltpu.VMEM(esum.shape, F32), pltpu.SemaphoreType.DMA],
        input_output_aliases={0: 0},
        compiler_params=pltpu.CompilerParams(vmem_limit_bytes=4 * MIB),
    )(out, esum, count, *parts)


def sent(block, slabs, distance):
    n, m = lax.axis_size("tm"), lax.axis_size("chan")
    if distance == 0:
        return lax.ppermute(block, "tm", [(i, (i + slabs) % n) for i in range(n)]) if slabs else block
    if slabs == 0:
        return lax.ppermute(block, "chan", [(k, k ^ distance) for k in range(m)])
    route = [(i * m + k, (i + slabs) % n * m + (k ^ distance)) for i in range(n) for k in range(m)]
    return lax.ppermute(block, ("tm", "chan"), route)


together = lax.optimization_barrier


def local(data, templates, valid):
    pieces = lax.axis_size("chan")
    n = lax.axis_size("tm")
    others = range(1, pieces // 2)
    head = lax.ppermute(edge_of(data), "tm", [(i + 1, i) for i in range(n - 1)])
    valid1 = sent(valid, -1, 0)
    valid2 = sent(valid, -2, 0)
    w, norm = tap_major(templates, valid)
    w, head, valid1, valid2, moving = together((w, head, valid1, valid2, data))
    earlier = sent(moving, 1, 0)
    earliest = sent(moving, 2, 0)

    power_keep, power_give = power_of(data, head, (valid, valid1, valid2), pieces)
    head, power_give = together((head, power_give))
    power_got = sent(power_give, 0, 1)

    keep0, give0 = correlated(w, norm, data, head, None, pieces)
    give0, power_got = together((give0, power_got))
    got0 = sent(give0, 0, 1)
    powers = [power_keep[d] + power_got[d] for d in others]
    earlier, _ = together((earlier, powers))
    powers = [sent(part, 0, 2 * d) for d, part in zip(others, powers)]

    keep1, give1 = correlated(w, norm, earlier, data, 0, pieces)
    give1, got0 = together((give1, got0))
    got1 = sent(give1, 0, 1)
    got1, powers = together((got1, powers))
    num0 = [keep0[d] + got0[d] for d in others]
    num1 = [keep1[d] + got1[d] for d in range(pieces // 2)]
    earliest, _, _ = together((earliest, num0, num1))
    num0 = [sent(part, 0, 2 * d) for d, part in zip(others, num0)]
    num1 = [sent(part, -1, 2 * d) for d, part in enumerate(num1)]

    keep2, give2 = correlated(w, norm, earliest, earlier, 1, pieces)
    give2, num1, num0 = together((give2, num1, num0))
    got2 = sent(give2, 0, 1)
    num2 = [keep2[d] + got2[d] for d in range(pieces // 2)]
    num2 = [sent(part, -2, 2 * d) for d, part in enumerate(num2)]
    out, esum, count = early([power_keep, power_got] + powers, [keep0, got0] + num0, num1)
    return last(out, esum, count, num2)


def solution(mesh):
    placed = (P("chan", "tm"), P("tm", "chan"), P("tm", "chan"))
    return jax.shard_map(
        local, mesh=mesh, in_specs=placed, out_specs=P(None, "chan", "tm"), check_vma=False
    )
```
